256 devices in a mesh: dp: 32 (over x, z), expert: 8 (over y, core).
Axes of the slice: x: 4, y: 4, z: 8, core: 2. Of those that a mesh axis runs over, the one named last changes fastest.
Arguments:
- teacher_in: bfloat16 [256, 6144], P('dp'), may hold values from -6 to 6
- route_ids: int32 [256, 2], replicated, may hold values from 0 to 7, all different within a row; in each aligned block of 8 rows (0 to 7, 8 to 15, ...) at most 4 rows name the same one
- router: bfloat16 [6144, 8], replicated, may hold values from -0.078125 to 0.078125
- w_gate: bfloat16 [8, 6144, 8192], P('expert', None, 'dp'), may hold values from -0.078125 to 0.078125
- w_up: bfloat16 [8, 6144, 8192], P('expert', None, 'dp'), may hold values from -0.078125 to 0.078125
- w_down: bfloat16 [8, 8192, 6144], P('expert', 'dp'), may hold values from -0.125 to 0.125
- projection: bfloat16 [6144, 4096], P('dp'), may hold values from -0.078125 to 0.078125
- student_in: bfloat16 [256, 4096], P('dp', 'expert'), may hold values from -6 to 6
- s_gate: bfloat16 [4096, 7168], P('expert', 'dp'), may hold values from -0.09375 to 0.09375
- s_up: bfloat16 [4096, 7168], P('expert', 'dp'), may hold values from -0.09375 to 0.09375
- s_down: bfloat16 [7168, 4096], P('dp', 'expert'), may hold values from -0.0625 to 0.0625
Outputs:
- grad_gate: bfloat16 [4096, 7168], P('expert', 'dp')
- grad_up: bfloat16 [4096, 7168], P('expert', 'dp')
- grad_down: bfloat16 [7168, 4096], P('dp', 'expert')
- mismatch: float32 [256, 4096], P('dp', 'expert')
The draws below stay inside these ranges and needn't reach their ends.
Inputs may be any that keep to these rules, and one draw needn't show every extreme that they name: `route_ids`: each row names two different experts. In every block of 8 rows (rows b * 8 to b * 8 + 7) no expert is named by more than 4 rows, and in some block an expert is named by exactly 4 rows.
All inputs are finite; a program needn't handle non-finite values.
Results may differ from the reference program's by a relative error of at most 0.011.
Values may be sent and summed in bfloat16 or wider, within the bound.
No kernel may reach another device: no remote copies, remote signals or barrier semaphores. Data moves between devices by JAX's collectives and lax.ppermute only.
A program may use at most 64 MiB of HBM per device.

```python
import math
import jax
import jax.numpy as jnp
import numpy as np
from jax import lax

D = 6144
HID = 8192
SD = 4096
SFF = 7168
TOK_DP = 8
EXPERTS = 8
TOKENS = 256
CAP = 4


def strengthened(result, key, source, target, parts, factor):
    owner, partner = [(jnp.arange(result.shape[axis_at]) // (result.shape[axis_at] // parts)).reshape([-1 if axis == axis_at else 1 for axis in range(result.ndim)]) for axis_at in (source, target)]
    chosen = jax.random.permutation(key, parts)[partner]
    strong = (owner == chosen) | (owner == (partner + parts // 2) % parts)
    return jnp.where(strong, factor * result, result)


def shard_levels(key, extent, pieces, low, high):
    factor_of = 1.0
    for axis_at, shards_of in pieces:
        steps = jax.random.uniform(jax.random.fold_in(jax.random.fold_in(key, 6), axis_at), (shards_of,), jnp.float32, low / len(pieces), high / len(pieces))
        factor_of = factor_of * jnp.repeat(jnp.exp(steps), extent[axis_at] // shards_of).reshape((-1,) + (1,) * (len(extent) - 1 - axis_at))
    return factor_of


def routed_block(own_key, own, number, rows, number_of, top, bound, lean):
    order = jax.random.permutation(own_key, number_of)
    crowded, usual = portions_of(number_of, rows * top, bound, lean, True), portions_of(number_of, rows * top, bound, lean, False)
    places = jnp.arange(number_of)

    def named(lengths, turn):
        used = int((lengths > 0).sum())
        fixed = max(1, used // 4)
        shifted = fixed + (places - fixed + turn * (used - fixed)) % max(1, number_of - fixed)
        return jnp.zeros((number_of,), jnp.int32).at[order[jnp.where(places < fixed, places, shifted)]].set(jnp.asarray(lengths, jnp.int32))

    lengths = jnp.where(number % 4 == 0, named(crowded, number // 4), named(usual, number - number // 4 - 1))
    mixed = jax.random.permutation(jax.random.fold_in(own, 3), number_of)
    donor, sink = mixed[0:number_of // 2 * 2:2], mixed[1:number_of // 2 * 2:2]
    margin = jnp.minimum(lengths[donor] - 1, bound - lengths[sink]) // 2
    margin = jnp.where((donor == order[0]) | (sink == order[0]) | (lengths[sink] == 0), 0, jnp.maximum(margin, 0))
    shifted = jax.random.randint(jax.random.fold_in(own, 4), (number_of // 2,), 0, 1 << 20) % (margin + 1)
    lengths = lengths.at[donor].add(-shifted).at[sink].add(shifted)
    items = jnp.searchsorted(jnp.cumsum(lengths), jnp.arange(rows * top), side="right").astype(jnp.int32)
    listing = items.reshape(top, rows).T
    listing = listing[jax.random.permutation(jax.random.fold_in(own, 1), rows)]
    turn = jax.random.randint(jax.random.fold_in(own, 2), (rows, 1), 0, top)
    return jnp.take_along_axis(listing, (jnp.arange(top)[None, :] + turn) % top, axis=1)


def portions_of(number_of, total, reach, lean, full):
    loads = [(1 << 20) // math.isqrt(standing ** lean) + 1 for standing in range(1, number_of + 1)]
    largest = reach if full else min(reach, max(-(-total // number_of), total * loads[0] // sum(loads)))
    least = 1 if total - largest >= number_of - 1 else 0
    holding, rest = [largest] + [least] * (number_of - 1), total - largest - least * (number_of - 1)
    while rest > 0:
        movable = [i for i in range(1, number_of) if holding[i] < largest] or [i for i in range(1, number_of) if holding[i] < reach]
        mass, remaining = sum([loads[i] for i in movable]), rest
        for i in movable:
            extra = min(reach - holding[i], max(1, remaining * loads[i] // mass), rest)
            holding[i] = holding[i] + extra
            rest = rest - extra
    return np.array(holding)


def centred(stream_key, dims, spread, limit, split=(), kind=jnp.bfloat16):
    factor_of = shard_levels(stream_key, dims, split, -0.22, 0.18) if split else 1.0
    drawn = jax.random.normal(stream_key, dims, jnp.float32) * spread * factor_of
    return jnp.minimum(jnp.maximum(drawn, -limit), limit).astype(kind)


def noise_with(stream_key, dims, deviation, reach, cuts, heavy, kind=jnp.bfloat16):
    result = deviation * jax.random.normal(stream_key, dims, jnp.float32)
    if cuts:
        result = result * shard_levels(stream_key, dims, cuts, -0.22, 0.18)
    return jnp.clip(strengthened(result, jax.random.fold_in(stream_key, 3), *heavy), -reach, reach).astype(kind)


def setup_inputs(seed: int = 0) -> dict:
    seeds = jax.random.split(jax.random.key(seed), 12)
    teacher_in = centred(seeds[0], (TOKENS, D), 1.0, 6.0, ((0, 32),))
    route_ids_keys = jax.random.split(jax.random.fold_in(seeds[1], 1), TOKENS // TOK_DP)
    route_ids_turns = jax.random.permutation(jax.random.fold_in(seeds[1], 3), TOKENS // TOK_DP)
    route_ids = jax.vmap(lambda own, number: routed_block(jax.random.fold_in(seeds[1], 2), own, number, TOK_DP, EXPERTS, 2, CAP, 2))(route_ids_keys, route_ids_turns).reshape((TOKENS, 2))
    router = centred(seeds[2], (D, EXPERTS), D ** -0.5, 0.078125)
    w_gate = centred(seeds[3], (EXPERTS, D, HID), D ** -0.5, 0.078125, ((0, 8), (2, 32)))
    w_up = centred(seeds[4], (EXPERTS, D, HID), D ** -0.5, 0.078125, ((0, 8), (2, 32)))
    w_down = noise_with(seeds[5], (EXPERTS, HID, D), HID ** -0.5, 0.125, ((0, 8), (1, 32)), (1, 2, 32, 2.75))
    projection = centred(seeds[6], (D, SD), D ** -0.5, 0.078125, ((0, 32),))
    student_in = centred(seeds[7], (TOKENS, SD), 1.0, 6.0, ((0, 32), (1, 8)))
    s_gate = centred(seeds[8], (SD, SFF), SD ** -0.5, 0.09375, ((0, 8), (1, 32)))
    s_up = centred(seeds[9], (SD, SFF), SD ** -0.5, 0.09375, ((0, 8), (1, 32)))
    s_down = centred(seeds[10], (SFF, SD), SFF ** -0.5, 0.0625, ((0, 32), (1, 8)))
    return {"teacher_in": teacher_in, "route_ids": route_ids, "router": router, "w_gate": w_gate, "w_up": w_up, "w_down": w_down, "projection": projection, "student_in": student_in, "s_gate": s_gate, "s_up": s_up, "s_down": s_down}


def slot_numbers(block_ids, experts):
    count = block_ids.shape[0]
    onehot = (block_ids[:, :, None] == jnp.arange(experts, dtype=jnp.int32)[None, None, :]).astype(jnp.int32)
    flat = onehot.reshape(count * 2, experts)
    before = jnp.cumsum(flat, axis=0) - flat
    return lax.optimization_barrier(jnp.sum(before * flat, axis=1)).reshape(count, 2).astype(jnp.int32)

def reference(teacher_in, route_ids, router, w_gate, w_up, w_down, projection, student_in, s_gate, s_up, s_down):
    experts = router.shape[1]
    blocks = TOKENS // TOK_DP
    logits = jnp.dot(teacher_in, router, preferred_element_type=jnp.float32)
    picked = jnp.take_along_axis(logits, route_ids, axis=1)
    gates = jax.nn.sigmoid(picked - picked[:, ::-1])
    id_blocks = route_ids.reshape(blocks, TOK_DP, 2)
    slot_blocks = jax.vmap(lambda block_ids: slot_numbers(block_ids, experts))(id_blocks)
    input_blocks = teacher_in.reshape(blocks, TOK_DP, D).astype(jnp.float32)
    slot_range = jnp.arange(CAP, dtype=jnp.int32)

    def one_expert(expert_index):
        match = (id_blocks == expert_index)[:, None, :, :] & (slot_blocks[:, None, :, :] == slot_range[None, :, None, None])
        chosen = lax.optimization_barrier(jnp.sum(match.astype(jnp.int32), axis=3)).astype(jnp.float32)
        expert_rows = jnp.einsum('bct,btd->bcd', chosen, input_blocks).astype(jnp.bfloat16).reshape(blocks * CAP, D)
        gate_part = jnp.dot(expert_rows, w_gate[expert_index], preferred_element_type=jnp.float32)
        up_part = jnp.dot(expert_rows, w_up[expert_index], preferred_element_type=jnp.float32)
        expert_hidden = (gate_part * jax.nn.sigmoid(gate_part) * up_part).astype(jnp.bfloat16)
        expert_out = jnp.dot(expert_hidden, w_down[expert_index], preferred_element_type=jnp.float32).astype(jnp.bfloat16)
        return jnp.dot(expert_out, projection, preferred_element_type=jnp.float32).astype(jnp.bfloat16)
    expert_proj = lax.map(one_expert, jnp.arange(experts, dtype=jnp.int32))
    block_of = jnp.arange(TOKENS, dtype=jnp.int32) // TOK_DP
    row_index = (block_of[:, None] * CAP + slot_blocks.reshape(TOKENS, 2)).astype(jnp.int32)
    picked_rows = expert_proj[route_ids, row_index].astype(jnp.float32)
    target = lax.optimization_barrier(jnp.sum(gates[:, :, None] * picked_rows, axis=1))
    gate_s = jnp.dot(student_in, s_gate, preferred_element_type=jnp.float32)
    up_s = jnp.dot(student_in, s_up, preferred_element_type=jnp.float32)
    sigma = jax.nn.sigmoid(gate_s)
    active = gate_s * sigma
    hidden_s = (active * up_s).astype(jnp.bfloat16)
    student_out = jnp.dot(hidden_s, s_down, preferred_element_type=jnp.float32)
    mismatch = student_in.astype(jnp.float32) + student_out - target
    cotangent = (mismatch * (1.0 / math.sqrt(TOKENS))).astype(jnp.bfloat16)
    grad_down = jnp.dot(hidden_s.T, cotangent, preferred_element_type=jnp.float32).astype(jnp.bfloat16)
    d_hidden = jnp.dot(cotangent, s_down.T, preferred_element_type=jnp.float32)
    d_gate = (d_hidden * up_s * sigma * (1.0 + gate_s * (1.0 - sigma))).astype(jnp.bfloat16)
    d_up = (d_hidden * active).astype(jnp.bfloat16)
    grad_gate = jnp.dot(student_in.T, d_gate, preferred_element_type=jnp.float32).astype(jnp.bfloat16)
    grad_up = jnp.dot(student_in.T, d_up, preferred_element_type=jnp.float32).astype(jnp.bfloat16)
    return (grad_gate, grad_up, grad_down, mismatch)
```

```python
import math

import jax
import jax.numpy as jnp
from jax import lax
from jax.sharding import Mesh
from jax.sharding import PartitionSpec as P

NX, NZ, NY, NC = 4, 8, 4, 2
DP = ("x", "z")
EX = ("y", "c")
BF = jnp.bfloat16
F32 = jnp.float32


def exchange(values, axes):
    return lax.all_to_all(values, axes, 0, 0, tiled=False)


def spread(values, axes, count):
    return exchange(jnp.broadcast_to(values[None], (count,) + values.shape), axes)


def swap_cores(values):
    return lax.ppermute(values, "c", [(0, 1), (1, 0)])


def both_cores(values, core):
    other = swap_cores(values)
    first = jnp.where(core == 0, values, other)
    second = jnp.where(core == 0, other, values)
    return first, second


def expert_sum(values):
    rows, width = values.shape
    terms = exchange(values.astype(BF).reshape(NY * NC, rows // (NY * NC), width), EX)
    mine = jnp.sum(terms.astype(F32), axis=0)
    return spread(mine.astype(BF), EX, NY * NC).reshape(rows, width).astype(F32)


def body(
    teacher_in,
    route_ids,
    router,
    w_gate,
    w_up,
    w_down,
    projection,
    student_in,
    s_gate,
    s_up,
    s_down,
):
    core = lax.axis_index("c")
    row = lax.axis_index("y")
    expert = row * NC + core
    tok_dp, width = teacher_in.shape
    tokens = route_ids.shape[0]
    experts = router.shape[1]
    sff_dev = s_gate.shape[1]
    sd_dev = student_in.shape[1]
    chunk = width // (NY * NC)

    part = lax.dynamic_slice_in_dim(teacher_in, expert * chunk, chunk, 1)
    column = spread(part, "z", NZ).reshape(NZ * tok_dp, chunk)
    plane = spread(column, ("x", "y"), NX * NY).reshape(NX, NY, NZ * tok_dp, chunk)
    even, odd = both_cores(plane, core)
    every = jnp.stack([even, odd], axis=0)
    every = every.transpose(1, 3, 2, 0, 4).reshape(tokens, width)

    logits = jnp.dot(every, router, preferred_element_type=F32)
    lane = lax.broadcasted_iota(jnp.int32, (tokens, experts), 1)
    first = route_ids[:, 0:1]
    second = route_ids[:, 1:2]
    l0 = jnp.sum(jnp.where(lane == first, logits, 0.0), axis=1, keepdims=True)
    l1 = jnp.sum(jnp.where(lane == second, logits, 0.0), axis=1, keepdims=True)
    gate = jnp.where(first == expert, jax.nn.sigmoid(l0 - l1), 0.0) + jnp.where(
        second == expert, jax.nn.sigmoid(l1 - l0), 0.0
    )
    named = (first == expert) | (second == expert)

    gate_part = jnp.dot(every, w_gate[0], preferred_element_type=F32)
    up_part = jnp.dot(every, w_up[0], preferred_element_type=F32)
    active = gate_part * jax.nn.sigmoid(gate_part) * up_part
    hidden = jnp.where(named, active * gate, 0.0).astype(BF)

    partial = lax.dot_general(
        w_down[0], hidden, (((0,), (1,)), ((), ())), preferred_element_type=F32
    )
    half = tokens // NC
    low = partial[:, :half]
    high = partial[:, half:]
    keep = jnp.where(core == 0, low, high)
    give = jnp.where(core == 0, high, low).astype(BF)
    pair = (keep + swap_cores(give).astype(F32)).astype(BF)
    group = width // (NX * NZ * NY)
    terms = pair.reshape(NX, NZ, NY, group, half).transpose(0, 2, 1, 3, 4)
    terms = exchange(terms.reshape(NX * NY, NZ, group, half), ("x", "y"))
    summed = jnp.sum(terms.astype(F32), axis=0).astype(BF)
    terms = exchange(summed, "z")
    summed = jnp.sum(terms.astype(F32), axis=0).astype(BF)
    mine = spread(summed, EX, NY * NC)
    mine = mine.reshape(NY, NC, group, half).transpose(0, 2, 1, 3)
    mine = mine.reshape(NY * group, tokens)
    return_cols = lax.dynamic_slice_in_dim(projection, expert * sd_dev, sd_dev, 1)
    target = lax.dot_general(
        mine, return_cols, (((0,), (0,)), ((), ())), preferred_element_type=F32
    )

    student_all = spread(student_in, DP, NX * NZ).reshape(tokens, sd_dev)
    gate_s = jnp.dot(student_all, s_gate, preferred_element_type=F32)
    up_s = jnp.dot(student_all, s_up, preferred_element_type=F32)
    pair_sums = expert_sum(jnp.concatenate([gate_s, up_s], axis=1))
    gate_s = pair_sums[:, :sff_dev]
    up_s = pair_sums[:, sff_dev:]
    sigma = jax.nn.sigmoid(gate_s)
    active_s = gate_s * sigma
    hidden_s = (active_s * up_s).astype(BF)
    out_part = jnp.dot(hidden_s, s_down, preferred_element_type=F32) - target
    terms = exchange(out_part.astype(BF).reshape(NX * NZ, tok_dp, sd_dev), DP)
    mismatch = student_in.astype(F32) + jnp.sum(terms.astype(F32), axis=0)
    cotangent = (mismatch * (1.0 / math.sqrt(tokens))).astype(BF)
    cotangent_all = spread(cotangent, DP, NX * NZ).reshape(tokens, sd_dev)
    grad_down = lax.dot_general(
        hidden_s, cotangent_all, (((0,), (0,)), ((), ())), preferred_element_type=F32
    ).astype(BF)
    d_hidden = expert_sum(
        lax.dot_general(
            cotangent_all, s_down, (((1,), (1,)), ((), ())), preferred_element_type=F32
        )
    )
    d_gate = (d_hidden * up_s * sigma * (1.0 + gate_s * (1.0 - sigma))).astype(BF)
    d_up = (d_hidden * active_s).astype(BF)
    grad_gate = lax.dot_general(
        student_all, d_gate, (((0,), (0,)), ((), ())), preferred_element_type=F32
    ).astype(BF)
    grad_up = lax.dot_general(
        student_all, d_up, (((0,), (0,)), ((), ())), preferred_element_type=F32
    ).astype(BF)
    return (grad_gate, grad_up, grad_down, mismatch)


def solution(mesh):
    fine = Mesh(mesh.devices.reshape(NX, NZ, NY, NC), ("x", "z", "y", "c"))
    return jax.shard_map(
        body,
        mesh=fine,
        in_specs=(
            P(DP, None),
            P(),
            P(),
            P(EX, None, DP),
            P(EX, None, DP),
            P(EX, DP, None),
            P(DP, None),
            P(DP, EX),
            P(EX, DP),
            P(EX, DP),
            P(DP, EX),
        ),
        out_specs=(P(EX, DP), P(EX, DP), P(DP, EX), P(DP, EX)),
        check_vma=False,
    )
```

```python
import functools
import math

import jax
import jax.numpy as jnp
from jax import lax
from jax.experimental import pallas as pl
from jax.experimental.pallas import tpu as pltpu
from jax.sharding import Mesh
from jax.sharding import PartitionSpec as P

NX, NZ, NY, NC = 4, 8, 4, 2
ND = NX * NZ
NE = NY * NC
DP = ("x", "z")
EX = ("y", "c")
BF = jnp.bfloat16
F32 = jnp.float32
VMEM_BYTES = 28 * 1024 * 1024
STEPS = 8


def exchange(values, axes):
    return lax.all_to_all(values, axes, 0, 0, tiled=False)


def spread(values, axes, count):
    return exchange(jnp.broadcast_to(values[None], (count,) + values.shape), axes)


def swap_cores(values):
    return lax.ppermute(values, "c", [(0, 1), (1, 0)])


def along_y(values, shift):
    return lax.ppermute(values, "y", [(i, (i + shift) % NY) for i in range(NY)])


def expert_sum(values, core):
    half = values.shape[0] // 2
    low, high = values[:half], values[half:]
    give = jnp.where(core == 0, high, low).astype(BF)
    keep = jnp.where(core == 0, low, high)
    mine = (keep + swap_cores(give).astype(F32)).astype(BF)
    others = [along_y(mine, s) for s in range(1, NY)]
    total = mine.astype(F32)
    for term in others:
        total = total + term.astype(F32)
    total = total.astype(BF)
    other = swap_cores(total)
    first = jnp.where(core == 0, total, other)
    second = jnp.where(core == 0, other, total)
    return jnp.concatenate([first, second], axis=0).astype(F32)


def dot(a, b):
    return jnp.dot(a, b, preferred_element_type=F32)


def dot_tn(a, b):
    return lax.dot_general(a, b, (((0,), (0,)), ((), ())), preferred_element_type=F32)


def dot_nt(a, b):
    return lax.dot_general(a, b, (((1,), (1,)), ((), ())), preferred_element_type=F32)


def own_kernel(where_ref, x0, x1, wg, wu, rt, gate_out, up_out, logit_out):
    step = pl.program_id(0)

    @pl.when(step == 0)
    def _():
        x = x0[...]
        gate_out[...] = dot(x, wg[0])
        up_out[...] = dot(x, wu[0])
        logit_out[...] = dot(x, rt[...])

    @pl.when(step == 1)
    def _():
        x = x1[...]
        gate_out[...] += dot(x, wg[0])
        up_out[...] += dot(x, wu[0])
        logit_out[...] += dot(x, rt[...])


def rest_kernel(where_ref, *refs):
    xs = refs[:6]
    wg, wu, rt, gate_in, up_in, logit_in, ids, wd = refs[6:14]
    keeps = refs[14:18]
    gives = refs[18:22]
    gate_acc, up_acc, logit_acc, hidden, block = refs[22:]
    step = pl.program_id(0)
    row = where_ref[6]
    core = where_ref[7]

    for j in range(6):

        @pl.when(step == j)
        def _(j=j):
            x = xs[j][...]
            if j == 0:
                gate_acc[...] = gate_in[...] + dot(x, wg[0])
                up_acc[...] = up_in[...] + dot(x, wu[0])
                logit_acc[...] = logit_in[...] + dot(x, rt[...])
            else:
                gate_acc[...] += dot(x, wg[0])
                up_acc[...] += dot(x, wu[0])
                logit_acc[...] += dot(x, rt[...])

    @pl.when(step == 5)
    def _():
        expert = row * NC + core
        logits = logit_acc[...]
        lane = lax.broadcasted_iota(jnp.int32, logits.shape, 1)
        first = ids[:, 0:1]
        second = ids[:, 1:2]
        l0 = jnp.sum(jnp.where(lane == first, logits, 0.0), axis=1, keepdims=True)
        l1 = jnp.sum(jnp.where(lane == second, logits, 0.0), axis=1, keepdims=True)
        gate = jnp.where(first == expert, jax.nn.sigmoid(l0 - l1), 0.0) + jnp.where(
            second == expert, jax.nn.sigmoid(l1 - l0), 0.0
        )
        named = (first == expert) | (second == expert)
        g = gate_acc[...]
        active = g * jax.nn.sigmoid(g) * up_acc[...] * gate
        hidden[...] = jnp.where(named, active, 0.0).astype(BF)

    @pl.when(step >= 6)
    def _():
        res = dot_nt(wd[...], hidden[...])
        block[...] = res.reshape(block.shape)
        half = block.shape[3] // 2
        for s in range(NY):
            at = lax.rem(row + s, NY)
            low = block[:, at, :, :half]
            high = block[:, at, :, half:]
            keeps[s][...] = jnp.where(core == 0, low, high).astype(BF)
            gives[s][...] = jnp.where(core == 0, high, low).astype(BF)


def expert_own(where, x0, x1, w_gate, w_up, router, tokens, chunk):
    hid = w_gate.shape[2]
    experts = router.shape[1]
    whole = lambda i, w: (0, 0)
    return pl.pallas_call(
        own_kernel,
        out_shape=(
            jax.ShapeDtypeStruct((tokens, hid), F32),
            jax.ShapeDtypeStruct((tokens, hid), F32),
            jax.ShapeDtypeStruct((tokens, experts), F32),
        ),
        grid_spec=pltpu.PrefetchScalarGridSpec(
            num_scalar_prefetch=1,
            grid=(2,),
            in_specs=[
                pl.BlockSpec((tokens, chunk), whole),
                pl.BlockSpec((tokens, chunk), whole),
                pl.BlockSpec((1, chunk, hid), lambda i, w: (0, w[i], 0)),
                pl.BlockSpec((1, chunk, hid), lambda i, w: (0, w[i], 0)),
                pl.BlockSpec((chunk, experts), lambda i, w: (w[i], 0)),
            ],
            out_specs=[
                pl.BlockSpec((tokens, hid), whole),
                pl.BlockSpec((tokens, hid), whole),
                pl.BlockSpec((tokens, experts), whole),
            ],
        ),
        compiler_params=pltpu.CompilerParams(vmem_limit_bytes=VMEM_BYTES),
        cost_estimate=pl.CostEstimate(
            flops=4 * tokens * 2 * chunk * hid,
            bytes_accessed=4 * chunk * (2 * hid + tokens) + 8 * tokens * hid,
            transcendentals=0,
        ),
    )(where, x0, x1, w_gate, w_up, router)


def expert_rest(where, xs, w_gate, w_up, router, sums, ids, down_t, tokens, chunk):
    hid = w_gate.shape[2]
    experts = router.shape[1]
    width = down_t.shape[0]
    group = width // (ND * NY)
    rows = width // STEPS
    whole = lambda i, w: (0, 0)
    at = lambda i, w: w[jnp.minimum(i, 5)]
    late = lambda i: jnp.maximum(i - 6, 0)
    out = jax.ShapeDtypeStruct((ND, group, tokens // 2), BF)
    return pl.pallas_call(
        rest_kernel,
        out_shape=(out,) * 8,
        grid_spec=pltpu.PrefetchScalarGridSpec(
            num_scalar_prefetch=1,
            grid=(6 + STEPS,),
            in_specs=[pl.BlockSpec((tokens, chunk), whole)] * 6
            + [
                pl.BlockSpec((1, chunk, hid), lambda i, w: (0, at(i, w), 0)),
                pl.BlockSpec((1, chunk, hid), lambda i, w: (0, at(i, w), 0)),
                pl.BlockSpec((chunk, experts), lambda i, w: (at(i, w), 0)),
                pl.BlockSpec((tokens, hid), whole),
                pl.BlockSpec((tokens, hid), whole),
                pl.BlockSpec((tokens, experts), whole),
                pl.BlockSpec((tokens, 2), whole),
                pl.BlockSpec((rows, hid), lambda i, w: (late(i), 0)),
            ],
            out_specs=[
                pl.BlockSpec((ND // STEPS, group, tokens // 2), lambda i, w: (late(i), 0, 0))
            ]
            * 8,
            scratch_shapes=[
                pltpu.VMEM((tokens, hid), F32),
                pltpu.VMEM((tokens, hid), F32),
                pltpu.VMEM((tokens, experts), F32),
                pltpu.VMEM((tokens, hid), BF),
                pltpu.VMEM((ND // STEPS, NY, group, tokens), F32),
            ],
        ),
        compiler_params=pltpu.CompilerParams(vmem_limit_bytes=VMEM_BYTES),
        cost_estimate=pl.CostEstimate(
            flops=4 * tokens * 6 * chunk * hid + 2 * tokens * hid * width,
            bytes_accessed=12 * chunk * (2 * hid + tokens) + 2 * width * (hid + tokens),
            transcendentals=tokens * hid,
        ),
    )(where, *xs, w_gate, w_up, router, *sums, ids, down_t)


def body(
    teacher_in,
    route_ids,
    router,
    w_gate,
    w_up,
    w_down,
    projection,
    student_in,
    s_gate,
    s_up,
    s_down,
):
    core = lax.axis_index("c")
    row = lax.axis_index("y")
    expert = row * NC + core
    tok_dp, width = teacher_in.shape
    tokens = route_ids.shape[0]
    sff_dev = s_gate.shape[1]
    sd_dev = student_in.shape[1]
    chunk = width // NE
    half = tokens // 2
    group = width // (ND * NY)

    part = lax.dynamic_slice_in_dim(teacher_in, expert * chunk, chunk, 1)
    sent = jnp.concatenate([part, student_in], axis=1)
    arrived = spread(sent, DP, ND).reshape(tokens, chunk + sd_dev)
    own = arrived[:, :chunk]
    student_all = arrived[:, chunk:]
    down_t = w_down[0].T

    far = [along_y(own, s) for s in range(1, NY)]
    own_other = swap_cores(own)
    far_other = [swap_cores(v) for v in far]

    def places(shift):
        r = lax.rem(row - shift + NY, NY)
        return [r * NC + core, r * NC + 1 - core]

    here = jnp.stack(places(0)).astype(jnp.int32)
    sums = expert_own(here, own, own_other, w_gate, w_up, router, tokens, chunk)
    xs, spots = [], []
    for s in (1, 3, 2):
        xs += [far[s - 1], far_other[s - 1]]
        spots += places(s)
    there = jnp.stack(spots + [row, core]).astype(jnp.int32)
    parts = expert_rest(
        there, xs, w_gate, w_up, router, sums, route_ids, down_t, tokens, chunk
    )
    keeps, gives = parts[:4], parts[4:]

    pair_sums = expert_sum(
        jnp.concatenate([dot(student_all, s_gate), dot(student_all, s_up)], axis=1), core
    )
    gate_s = pair_sums[:, :sff_dev]
    up_s = pair_sums[:, sff_dev:]
    sigma = jax.nn.sigmoid(gate_s)
    active_s = gate_s * sigma
    hidden_s = (active_s * up_s).astype(BF)
    student_part = dot(hidden_s, s_down)

    arriving = []
    mine = None
    for s in (2, 1, 3, 0):
        both = (keeps[s].astype(F32) + swap_cores(gives[s]).astype(F32)).astype(BF)
        if s:
            arriving.append(along_y(both, s))
        else:
            mine = both
    total = mine.astype(F32)
    for term in arriving:
        total = total + term.astype(F32)
    terms = exchange(total.astype(BF), DP)
    summed = jnp.sum(terms.astype(F32), axis=0).astype(BF)
    pieces = [summed] + [along_y(summed, s) for s in range(1, NY)]
    mine = jnp.concatenate(pieces, axis=0)
    other = swap_cores(mine)
    cols = lax.dynamic_slice_in_dim(projection, expert * sd_dev, sd_dev, 1)
    cols = jnp.concatenate(
        [
            lax.dynamic_slice_in_dim(cols, lax.rem(row - s + NY, NY) * group, group, 0)
            for s in range(NY)
        ],
        axis=0,
    )
    first = jnp.where(core == 0, mine, other)
    second = jnp.where(core == 0, other, mine)
    target = dot_tn(jnp.concatenate([first, second], axis=1), cols)

    out_part = (student_part - target).astype(BF)
    terms = exchange(out_part.reshape(ND, tok_dp, sd_dev), DP)
    mismatch = student_in.astype(F32) + jnp.sum(terms.astype(F32), axis=0)
    cotangent = (mismatch * (1.0 / math.sqrt(tokens))).astype(BF)
    cotangent_all = spread(cotangent, DP, ND).reshape(tokens, sd_dev)
    grad_down = dot_tn(hidden_s, cotangent_all).astype(BF)
    d_hidden = expert_sum(dot_nt(cotangent_all, s_down), core)
    d_gate = (d_hidden * up_s * sigma * (1.0 + gate_s * (1.0 - sigma))).astype(BF)
    d_up = (d_hidden * active_s).astype(BF)
    grad_gate = dot_tn(student_all, d_gate).astype(BF)
    grad_up = dot_tn(student_all, d_up).astype(BF)
    return (grad_gate, grad_up, grad_down, mismatch)


def solution(mesh):
    fine = Mesh(mesh.devices.reshape(NX, NZ, NY, NC), ("x", "z", "y", "c"))
    return jax.shard_map(
        body,
        mesh=fine,
        in_specs=(
            P(DP, None),
            P(),
            P(),
            P(EX, None, DP),
            P(EX, None, DP),
            P(EX, DP, None),
            P(DP, None),
            P(DP, EX),
            P(EX, DP),
            P(EX, DP),
            P(DP, EX),
        ),
        out_specs=(P(EX, DP), P(EX, DP), P(DP, EX), P(DP, EX)),
        check_vma=False,
    )
```

```python
import math

import jax
import jax.numpy as jnp
from jax import lax
from jax.experimental import pallas as pl
from jax.experimental.pallas import tpu as pltpu
from jax.sharding import Mesh
from jax.sharding import PartitionSpec as P

NX, NZ, NY, NC = 4, 8, 4, 2
ND = NX * NZ
NE = NY * NC
DP = ("x", "z")
EX = ("y", "c")
BF = jnp.bfloat16
F32 = jnp.float32
VMEM_BYTES = 60 * 1024 * 1024
STEPS = 4


def exchange(values, axes):
    return lax.all_to_all(values, axes, 0, 0, tiled=False)


def spread(values, axes, count):
    return exchange(jnp.broadcast_to(values[None], (count,) + values.shape), axes)


def swap_cores(values):
    return lax.ppermute(values, "c", [(0, 1), (1, 0)])


def along_y(values, shift):
    return lax.ppermute(values, "y", [(i, (i + shift) % NY) for i in range(NY)])


def core_sum(values, core):
    half = values.shape[0] // 2
    low, high = values[:half], values[half:]
    give = jnp.where(core == 0, high, low).astype(BF)
    keep = jnp.where(core == 0, low, high)
    return (keep + swap_cores(give).astype(F32)).astype(BF)


def row_sum(mine, beside):
    others = [along_y(mine, s) for s in range(1, NY)]
    others, beside = lax.optimization_barrier((others, beside))
    total = mine.astype(F32)
    for term in others:
        total = total + term.astype(F32)
    total = total.astype(BF)
    return total, swap_cores(total), beside


def in_order(mine, other, core):
    first = jnp.where(core == 0, mine, other)
    second = jnp.where(core == 0, other, mine)
    return jnp.concatenate([first, second], axis=0)


def dot(a, b):
    return jnp.dot(a, b, preferred_element_type=F32)


def dot_tn(a, b):
    return lax.dot_general(a, b, (((0,), (0,)), ((), ())), preferred_element_type=F32)


def dot_nt(a, b):
    return lax.dot_general(a, b, (((1,), (1,)), ((), ())), preferred_element_type=F32)


def two_parts(core, chunk):
    mine = pl.multiple_of(core * chunk, 256)
    rest = pl.multiple_of((1 - core) * chunk, 256)
    return pl.ds(mine, chunk), pl.ds(rest, chunk)


def weight_copies(where_ref, j, hbm_refs, buffers, sems):
    depth = buffers[0].shape[1]
    start = pl.multiple_of(where_ref[j] * depth, 512)
    return [
        pltpu.make_async_copy(src.at[0, pl.ds(start, depth), :], buf.at[j], sems.at[i, j])
        for i, (src, buf) in enumerate(zip(hbm_refs, buffers))
    ]


def products(a, b, spot, wg, wu, rt, core):
    chunk = a.shape[1]
    mine, rest = two_parts(core, chunk)
    base = spot * (2 * chunk)
    r0 = rt[:, pl.ds(pl.multiple_of(base + core * chunk, 256), chunk)]
    r1 = rt[:, pl.ds(pl.multiple_of(base + (1 - core) * chunk, 256), chunk)]
    return (
        dot(a, wg[mine, :]) + dot(b, wg[rest, :]),
        dot(a, wu[mine, :]) + dot(b, wu[rest, :]),
        dot_nt(a, r0) + dot_nt(b, r1),
    )


def expert_kernel(where, *refs):
    xs = refs[:8]
    wg, wu, rt, ids, wd = refs[8:13]
    keeps = refs[13:17]
    gives = refs[17:21]
    gbuf, ubuf, dbuf, hidden, block, sems, dsems = refs[21:]
    row = where[0]
    core = where[NY]
    copies = [weight_copies(where, j, (wg, wu), (gbuf, ubuf), sems) for j in range(NY)]
    rows = dbuf.shape[1]
    downs = [
        pltpu.make_async_copy(wd.at[pl.ds(j * rows, rows), :], dbuf.at[j], dsems.at[j])
        for j in range(STEPS)
    ]
    for group in copies:
        for copy in group:
            copy.start()
    for copy in downs:
        copy.start()
    g = u = logits = None
    for j in range(NY):
        for copy in copies[j]:
            copy.wait()
        gate, up, logit = products(
            xs[2 * j][...], xs[2 * j + 1][...], where[j], gbuf.at[j], ubuf.at[j], rt, core
        )
        if j == 0:
            g, u, logits = gate, up, logit
        else:
            g, u, logits = g + gate, u + up, logits + logit

    expert = row * NC + core
    lane = lax.broadcasted_iota(jnp.int32, logits.shape, 1)
    first = ids[:, 0:1]
    second = ids[:, 1:2]
    l0 = jnp.sum(jnp.where(lane == first, logits, 0.0), axis=1, keepdims=True)
    l1 = jnp.sum(jnp.where(lane == second, logits, 0.0), axis=1, keepdims=True)
    gate = jnp.where(first == expert, jax.nn.sigmoid(l0 - l1), 0.0) + jnp.where(
        second == expert, jax.nn.sigmoid(l1 - l0), 0.0
    )
    named = (first == expert) | (second == expert)
    active = jnp.where(named, g * jax.nn.sigmoid(g) * u * gate, 0.0)
    half = active.shape[0] // 2
    low = active[:half]
    high = active[half:]
    hidden[:half] = jnp.where(core == 0, low, high).astype(BF)
    hidden[half:] = jnp.where(core == 0, high, low).astype(BF)

    count = block.shape[0]
    for j in range(STEPS):
        downs[j].wait()
        res = dot_nt(dbuf[j], hidden[...])
        block[...] = res.astype(BF).reshape(block.shape)
        for s in range(NY):
            at = lax.rem(row + s, NY)
            keeps[s][j * count : (j + 1) * count] = block[:, at, :, :half]
            gives[s][j * count : (j + 1) * count] = block[:, at, :, half:]


IN_SMEM = pl.BlockSpec(memory_space=pltpu.SMEM)
IN_VMEM = pl.BlockSpec(memory_space=pltpu.VMEM)
IN_HBM = pl.BlockSpec(memory_space=pltpu.HBM)


def expert_products(where, xs, w_gate, w_up, router_t, ids, down_t, tokens, chunk):
    hid = w_gate.shape[2]
    width = down_t.shape[0]
    group = width // (ND * NY)
    out = jax.ShapeDtypeStruct((ND, group, tokens // 2), BF)
    return pl.pallas_call(
        expert_kernel,
        out_shape=(out,) * 8,
        in_specs=[IN_SMEM]
        + [IN_VMEM] * 8
        + [IN_HBM, IN_HBM, IN_VMEM, IN_VMEM, IN_HBM],
        out_specs=[IN_VMEM] * 8,
        scratch_shapes=[
            pltpu.VMEM((NY, 2 * chunk, hid), BF),
            pltpu.VMEM((NY, 2 * chunk, hid), BF),
            pltpu.VMEM((STEPS, width // STEPS, hid), BF),
            pltpu.VMEM((tokens, hid), BF),
            pltpu.VMEM((ND // STEPS, NY, group, tokens), BF),
            pltpu.SemaphoreType.DMA((2, NY)),
            pltpu.SemaphoreType.DMA((STEPS,)),
        ],
        compiler_params=pltpu.CompilerParams(vmem_limit_bytes=VMEM_BYTES),
        cost_estimate=pl.CostEstimate(
            flops=4 * tokens * NE * chunk * hid + 2 * tokens * hid * width,
            bytes_accessed=2 * NE * chunk * (2 * hid + tokens) + 2 * width * (hid + tokens),
            transcendentals=tokens * hid,
        ),
    )(where, *xs, w_gate, w_up, router_t, ids, down_t)


def grad_kernel(core_ref, own, other, gate, up, student, gate_grad, up_grad):
    half = own.shape[0]
    core = core_ref[0]
    total_gate = None
    for side, d_ref in enumerate((own, other)):
        at = core if side == 0 else 1 - core
        rows = pl.ds(pl.multiple_of(at * half, 128), half)
        d_hidden = d_ref[...].astype(F32)
        g = gate[rows, :]
        sigma = jax.nn.sigmoid(g)
        d_gate = (d_hidden * up[rows, :] * sigma * (1.0 + g * (1.0 - sigma))).astype(BF)
        d_up = (d_hidden * (g * sigma)).astype(BF)
        tokens = student[rows, :]
        if side == 0:
            total_gate = dot_tn(d_gate, tokens)
            total_up = dot_tn(d_up, tokens)
        else:
            gate_grad[...] = (total_gate + dot_tn(d_gate, tokens)).astype(BF)
            up_grad[...] = (total_up + dot_tn(d_up, tokens)).astype(BF)


def weight_grads(core, own, other, gate_s, up_s, student_all):
    out = jax.ShapeDtypeStruct((gate_s.shape[1], student_all.shape[1]), BF)
    return pl.pallas_call(
        grad_kernel,
        out_shape=(out, out),
        in_specs=[pl.BlockSpec(memory_space=pltpu.SMEM)]
        + [pl.BlockSpec(memory_space=pltpu.VMEM)] * 5,
        out_specs=[pl.BlockSpec(memory_space=pltpu.VMEM)] * 2,
        compiler_params=pltpu.CompilerParams(vmem_limit_bytes=16 * 1024 * 1024),
    )(core, own, other, gate_s, up_s, student_all)


def body(
    teacher_in,
    route_ids,
    router,
    w_gate,
    w_up,
    w_down,
    projection,
    student_in,
    s_gate,
    s_up,
    s_down,
):
    core = lax.axis_index("c")
    row = lax.axis_index("y")
    expert = row * NC + core
    tok_dp, width = teacher_in.shape
    tokens = route_ids.shape[0]
    sff_dev = s_gate.shape[1]
    sd_dev = student_in.shape[1]
    chunk = width // NE
    half = tokens // 2
    group = width // (ND * NY)

    part = lax.dynamic_slice_in_dim(teacher_in, expert * chunk, chunk, 1)
    sent = jnp.concatenate([part, student_in], axis=1)
    arrived = spread(sent, DP, ND).reshape(tokens, chunk + sd_dev)
    arrived, down_t = lax.optimization_barrier((arrived, w_down[0].T))
    own = arrived[:, :chunk]
    student_all = arrived[:, chunk:]
    router_t = router.T

    far = [along_y(own, s) for s in range(1, NY)]
    own_other = swap_cores(own)
    far_other = [swap_cores(v) for v in far]
    xs, spots = [own, own_other], [row]
    for s in (1, 3, 2):
        xs += [far[s - 1], far_other[s - 1]]
        spots.append(lax.rem(row - s + NY, NY))
    where = jnp.stack(spots + [core]).astype(jnp.int32)
    parts = expert_products(
        where, xs, w_gate, w_up, router_t, route_ids, down_t, tokens, chunk
    )
    pair_mine = core_sum(
        jnp.concatenate([dot(student_all, s_gate), dot(student_all, s_up)], axis=1), core
    )
    keeps, gives = parts[:4], parts[4:]

    arriving = []
    mine = None
    for s in (2, 1, 3, 0):
        both = (keeps[s].astype(F32) + swap_cores(gives[s]).astype(F32)).astype(BF)
        if s:
            arriving.append(along_y(both, s))
        else:
            mine = both
    total = mine.astype(F32)
    for term in arriving:
        total = total + term.astype(F32)
    terms = exchange(total.astype(BF), DP)
    pair_mine, pair_other, _ = row_sum(pair_mine, row)
    pair_sums = in_order(pair_mine, pair_other, core).astype(F32)
    gate_s = pair_sums[:, :sff_dev]
    up_s = pair_sums[:, sff_dev:]
    hidden_s = (gate_s * jax.nn.sigmoid(gate_s) * up_s).astype(BF)
    student_part = dot(hidden_s, s_down)
    summed = jnp.sum(terms.astype(F32), axis=0).astype(BF)
    pieces = [summed] + [along_y(summed, s) for s in range(1, NY)]
    mine = jnp.concatenate(pieces, axis=0)
    other = swap_cores(mine)
    cols = lax.dynamic_slice_in_dim(projection, expert * sd_dev, sd_dev, 1)
    cols = jnp.concatenate(
        [
            lax.dynamic_slice_in_dim(cols, lax.rem(row - s + NY, NY) * group, group, 0)
            for s in range(NY)
        ],
        axis=0,
    )
    first = jnp.where(core == 0, mine, other)
    second = jnp.where(core == 0, other, mine)
    target = dot_tn(jnp.concatenate([first, second], axis=1), cols)

    out_part = (student_part - target).astype(BF)
    terms = exchange(out_part.reshape(ND, tok_dp, sd_dev), DP)
    mismatch = student_in.astype(F32) + jnp.sum(terms.astype(F32), axis=0)
    cotangent = (mismatch * (1.0 / math.sqrt(tokens))).astype(BF)
    cotangent_all = spread(cotangent, DP, ND).reshape(tokens, sd_dev)
    grad_down = dot_tn(hidden_s, cotangent_all).astype(BF)
    d_mine, d_other, grad_down = row_sum(
        core_sum(dot_nt(cotangent_all, s_down), core), grad_down
    )
    core_at = jnp.reshape(core, (1,)).astype(jnp.int32)
    grad_gate, grad_up = weight_grads(core_at, d_mine, d_other, gate_s, up_s, student_all)
    grad_gate = grad_gate.T
    grad_up = grad_up.T
    return (grad_gate, grad_up, grad_down, mismatch)


def solution(mesh):
    fine = Mesh(mesh.devices.reshape(NX, NZ, NY, NC), ("x", "z", "y", "c"))
    return jax.shard_map(
        body,
        mesh=fine,
        in_specs=(
            P(DP, None),
            P(),
            P(),
            P(EX, None, DP),
            P(EX, None, DP),
            P(EX, DP, None),
            P(DP, None),
            P(DP, EX),
            P(EX, DP),
            P(EX, DP),
            P(DP, EX),
        ),
        out_specs=(P(EX, DP), P(EX, DP), P(DP, EX), P(DP, EX)),
        check_vma=False,
    )
```

```python
import math

import jax
import jax.numpy as jnp
from jax import lax
from jax.experimental import pallas as pl
from jax.experimental.pallas import tpu as pltpu
from jax.sharding import Mesh
from jax.sharding import PartitionSpec as P

NX, NZ, NY, NC = 4, 8, 4, 2
ND = NX * NZ
NE = NY * NC
DP = ("x", "z")
EX = ("y", "c")
BF = jnp.bfloat16
F32 = jnp.float32
VMEM_BYTES = 60 * 1024 * 1024
STEPS = 4


def exchange(values, axes):
    return lax.all_to_all(values, axes, 0, 0, tiled=False)


def spread(values, axes, count):
    return exchange(jnp.broadcast_to(values[None], (count,) + values.shape), axes)


def swap_cores(values):
    return lax.ppermute(values, "c", [(0, 1), (1, 0)])


def along_y(values, shift):
    return lax.ppermute(values, "y", [(i, (i + shift) % NY) for i in range(NY)])


def core_sum(values, core):
    half = values.shape[0] // 2
    low, high = values[:half], values[half:]
    give = jnp.where(core == 0, high, low).astype(BF)
    keep = jnp.where(core == 0, low, high)
    return (keep + swap_cores(give).astype(F32)).astype(BF)


def row_sum(mine, beside):
    others = [along_y(mine, s) for s in range(1, NY)]
    others, beside = lax.optimization_barrier((others, beside))
    total = mine.astype(F32)
    for term in others:
        total = total + term.astype(F32)
    total = total.astype(BF)
    return total, swap_cores(total), beside


def in_order(mine, other, core):
    first = jnp.where(core == 0, mine, other)
    second = jnp.where(core == 0, other, mine)
    return jnp.concatenate([first, second], axis=0)


def dot(a, b):
    return jnp.dot(a, b, preferred_element_type=F32)


def dot_tn(a, b):
    return lax.dot_general(a, b, (((0,), (0,)), ((), ())), preferred_element_type=F32)


def dot_nt(a, b):
    return lax.dot_general(a, b, (((1,), (1,)), ((), ())), preferred_element_type=F32)


def two_parts(core, chunk):
    mine = pl.multiple_of(core * chunk, 256)
    rest = pl.multiple_of((1 - core) * chunk, 256)
    return pl.ds(mine, chunk), pl.ds(rest, chunk)


def weight_copies(where_ref, j, hbm_refs, buffers, sems):
    depth = buffers[0].shape[1]
    start = pl.multiple_of(where_ref[j] * depth, 512)
    return [
        pltpu.make_async_copy(src.at[0, pl.ds(start, depth), :], buf.at[j], sems.at[i, j])
        for i, (src, buf) in enumerate(zip(hbm_refs, buffers))
    ]


def products(a, b, spot, wg, wu, rt, core):
    chunk = a.shape[1]
    mine, rest = two_parts(core, chunk)
    base = spot * (2 * chunk)
    r0 = rt[:, pl.ds(pl.multiple_of(base + core * chunk, 256), chunk)]
    r1 = rt[:, pl.ds(pl.multiple_of(base + (1 - core) * chunk, 256), chunk)]
    return (
        dot(a, wg[mine, :]) + dot(b, wg[rest, :]),
        dot(a, wu[mine, :]) + dot(b, wu[rest, :]),
        dot_nt(a, r0) + dot_nt(b, r1),
    )


def expert_kernel(where, *refs):
    xs = refs[:8]
    wg, wu, rt, ids, wd = refs[8:13]
    keeps = refs[13:17]
    gives = refs[17:21]
    xbuf, gbuf, ubuf, dbuf, hidden, block, obuf, xsems, sems, dsems, osems = refs[21:]
    outs = tuple(keeps) + tuple(gives)
    row = where[0]
    core = where[NY]
    copies = [weight_copies(where, j, (wg, wu), (gbuf, ubuf), sems) for j in range(NY)]
    rows = dbuf.shape[1]
    downs = [
        pltpu.make_async_copy(wd.at[pl.ds(j * rows, rows), :], dbuf.at[j], dsems.at[j])
        for j in range(STEPS)
    ]
    arrivals = [
        pltpu.make_async_copy(xs[i], xbuf.at[i], xsems.at[i]) for i in range(len(xs))
    ]
    for j in range(NY):
        for copy in copies[j] + arrivals[2 * j : 2 * j + 2]:
            copy.start()
    for copy in downs:
        copy.start()
    g = u = logits = None
    for j in range(NY):
        for copy in copies[j] + arrivals[2 * j : 2 * j + 2]:
            copy.wait()
        gate, up, logit = products(
            xbuf[2 * j], xbuf[2 * j + 1], where[j], gbuf.at[j], ubuf.at[j], rt, core
        )
        if j == 0:
            g, u, logits = gate, up, logit
        else:
            g, u, logits = g + gate, u + up, logits + logit

    expert = row * NC + core
    lane = lax.broadcasted_iota(jnp.int32, logits.shape, 1)
    first = ids[:, 0:1]
    second = ids[:, 1:2]
    l0 = jnp.sum(jnp.where(lane == first, logits, 0.0), axis=1, keepdims=True)
    l1 = jnp.sum(jnp.where(lane == second, logits, 0.0), axis=1, keepdims=True)
    gate = jnp.where(first == expert, jax.nn.sigmoid(l0 - l1), 0.0) + jnp.where(
        second == expert, jax.nn.sigmoid(l1 - l0), 0.0
    )
    named = (first == expert) | (second == expert)
    active = jnp.where(named, g * jax.nn.sigmoid(g) * u * gate, 0.0)
    half = active.shape[0] // 2
    low = active[:half]
    high = active[half:]
    hidden[:half] = jnp.where(core == 0, low, high).astype(BF)
    hidden[half:] = jnp.where(core == 0, high, low).astype(BF)

    count = block.shape[0]
    leaving = []
    for j in range(STEPS):
        downs[j].wait()
        res = dot_nt(dbuf[j], hidden[...])
        block[...] = res.astype(BF).reshape(block.shape)
        span = pl.ds(j * count, count)
        for s in range(NY):
            at = lax.rem(row + s, NY)
            obuf[s, span] = block[:, at, :, :half]
            obuf[NY + s, span] = block[:, at, :, half:]
        for i in range(2 * NY):
            leave = pltpu.make_async_copy(
                obuf.at[i, span], outs[i].at[span], osems.at[i, j]
            )
            leave.start()
            leaving.append(leave)
    for leave in leaving:
        leave.wait()


IN_SMEM = pl.BlockSpec(memory_space=pltpu.SMEM)
IN_VMEM = pl.BlockSpec(memory_space=pltpu.VMEM)
IN_HBM = pl.BlockSpec(memory_space=pltpu.HBM)
IN_ANY = pl.BlockSpec(memory_space=pl.ANY)


def expert_products(where, xs, w_gate, w_up, router_t, ids, down_t, tokens, chunk):
    hid = w_gate.shape[2]
    width = down_t.shape[0]
    group = width // (ND * NY)
    out = jax.ShapeDtypeStruct((ND, group, tokens // 2), BF)
    return pl.pallas_call(
        expert_kernel,
        out_shape=(out,) * 8,
        in_specs=[IN_SMEM]
        + [IN_ANY] * 8
        + [IN_HBM, IN_HBM, IN_VMEM, IN_VMEM, IN_HBM],
        out_specs=[IN_ANY] * 8,
        scratch_shapes=[
            pltpu.VMEM((NE, tokens, chunk), BF),
            pltpu.VMEM((NY, 2 * chunk, hid), BF),
            pltpu.VMEM((NY, 2 * chunk, hid), BF),
            pltpu.VMEM((STEPS, width // STEPS, hid), BF),
            pltpu.VMEM((tokens, hid), BF),
            pltpu.VMEM((ND // STEPS, NY, group, tokens), BF),
            pltpu.VMEM((2 * NY, ND, group, tokens // 2), BF),
            pltpu.SemaphoreType.DMA((NE,)),
            pltpu.SemaphoreType.DMA((2, NY)),
            pltpu.SemaphoreType.DMA((STEPS,)),
            pltpu.SemaphoreType.DMA((2 * NY, STEPS)),
        ],
        compiler_params=pltpu.CompilerParams(vmem_limit_bytes=VMEM_BYTES),
        cost_estimate=pl.CostEstimate(
            flops=4 * tokens * NE * chunk * hid + 2 * tokens * hid * width,
            bytes_accessed=2 * NE * chunk * (2 * hid + tokens) + 2 * width * (hid + tokens),
            transcendentals=tokens * hid,
        ),
    )(where, *xs, w_gate, w_up, router_t, ids, down_t)


def grad_kernel(core_ref, own, other, gate, up, student, gate_grad, up_grad):
    half = own.shape[0]
    core = core_ref[0]
    total_gate = None
    for side, d_ref in enumerate((own, other)):
        at = core if side == 0 else 1 - core
        rows = pl.ds(pl.multiple_of(at * half, 128), half)
        d_hidden = d_ref[...].astype(F32)
        g = gate[rows, :]
        sigma = jax.nn.sigmoid(g)
        d_gate = (d_hidden * up[rows, :] * sigma * (1.0 + g * (1.0 - sigma))).astype(BF)
        d_up = (d_hidden * (g * sigma)).astype(BF)
        tokens = student[rows, :]
        if side == 0:
            total_gate = dot_tn(d_gate, tokens)
            total_up = dot_tn(d_up, tokens)
        else:
            gate_grad[...] = (total_gate + dot_tn(d_gate, tokens)).astype(BF)
            up_grad[...] = (total_up + dot_tn(d_up, tokens)).astype(BF)


def weight_grads(core, own, other, gate_s, up_s, student_all):
    out = jax.ShapeDtypeStruct((gate_s.shape[1], student_all.shape[1]), BF)
    return pl.pallas_call(
        grad_kernel,
        out_shape=(out, out),
        in_specs=[pl.BlockSpec(memory_space=pltpu.SMEM)]
        + [pl.BlockSpec(memory_space=pltpu.VMEM)] * 5,
        out_specs=[pl.BlockSpec(memory_space=pltpu.VMEM)] * 2,
        compiler_params=pltpu.CompilerParams(vmem_limit_bytes=16 * 1024 * 1024),
    )(core, own, other, gate_s, up_s, student_all)


def body(
    teacher_in,
    route_ids,
    router,
    w_gate,
    w_up,
    w_down,
    projection,
    student_in,
    s_gate,
    s_up,
    s_down,
):
    core = lax.axis_index("c")
    row = lax.axis_index("y")
    expert = row * NC + core
    tok_dp, width = teacher_in.shape
    tokens = route_ids.shape[0]
    sff_dev = s_gate.shape[1]
    sd_dev = student_in.shape[1]
    chunk = width // NE
    half = tokens // 2
    group = width // (ND * NY)

    part = lax.dynamic_slice_in_dim(teacher_in, expert * chunk, chunk, 1)
    sent = jnp.concatenate([part, student_in], axis=1)
    arrived = spread(sent, DP, ND).reshape(tokens, chunk + sd_dev)
    arrived, down_t = lax.optimization_barrier((arrived, w_down[0].T))
    own = arrived[:, :chunk]
    student_all = arrived[:, chunk:]
    router_t = router.T

    far = [along_y(own, s) for s in range(1, NY)]
    own_other = swap_cores(own)
    far_other = [swap_cores(v) for v in far]
    xs, spots = [own, own_other], [row]
    for s in (1, 3, 2):
        xs += [far[s - 1], far_other[s - 1]]
        spots.append(lax.rem(row - s + NY, NY))
    where = jnp.stack(spots + [core]).astype(jnp.int32)
    parts = expert_products(
        where, xs, w_gate, w_up, router_t, route_ids, down_t, tokens, chunk
    )
    pair_mine = core_sum(
        jnp.concatenate([dot(student_all, s_gate), dot(student_all, s_up)], axis=1), core
    )
    keeps, gives = parts[:4], parts[4:]

    arriving = []
    mine = None
    for s in (2, 1, 3, 0):
        both = (keeps[s].astype(F32) + swap_cores(gives[s]).astype(F32)).astype(BF)
        if s:
            arriving.append(along_y(both, s))
        else:
            mine = both
    total = mine.astype(F32)
    for term in arriving:
        total = total + term.astype(F32)
    terms = exchange(total.astype(BF), DP)
    pair_mine, pair_other, _ = row_sum(pair_mine, row)
    pair_sums = in_order(pair_mine, pair_other, core).astype(F32)
    gate_s = pair_sums[:, :sff_dev]
    up_s = pair_sums[:, sff_dev:]
    hidden_s = (gate_s * jax.nn.sigmoid(gate_s) * up_s).astype(BF)
    student_part = dot(hidden_s, s_down)
    summed = jnp.sum(terms.astype(F32), axis=0).astype(BF)
    pieces = [summed] + [along_y(summed, s) for s in range(1, NY)]
    mine = jnp.concatenate(pieces, axis=0)
    other = swap_cores(mine)
    cols = lax.dynamic_slice_in_dim(projection, expert * sd_dev, sd_dev, 1)
    cols = jnp.concatenate(
        [
            lax.dynamic_slice_in_dim(cols, lax.rem(row - s + NY, NY) * group, group, 0)
            for s in range(NY)
        ],
        axis=0,
    )
    first = jnp.where(core == 0, mine, other)
    second = jnp.where(core == 0, other, mine)
    target = dot_tn(jnp.concatenate([first, second], axis=1), cols)

    out_part = (student_part - target).astype(BF)
    terms = exchange(out_part.reshape(ND, tok_dp, sd_dev), DP)
    mismatch = student_in.astype(F32) + jnp.sum(terms.astype(F32), axis=0)
    cotangent = (mismatch * (1.0 / math.sqrt(tokens))).astype(BF)
    cotangent_all = spread(cotangent, DP, ND).reshape(tokens, sd_dev)
    grad_down = dot_tn(hidden_s, cotangent_all).astype(BF)
    d_mine, d_other, grad_down = row_sum(
        core_sum(dot_nt(cotangent_all, s_down), core), grad_down
    )
    core_at = jnp.reshape(core, (1,)).astype(jnp.int32)
    grad_gate, grad_up = weight_grads(core_at, d_mine, d_other, gate_s, up_s, student_all)
    grad_gate = grad_gate.T
    grad_up = grad_up.T
    return (grad_gate, grad_up, grad_down, mismatch)


def solution(mesh):
    fine = Mesh(mesh.devices.reshape(NX, NZ, NY, NC), ("x", "z", "y", "c"))
    return jax.shard_map(
        body,
        mesh=fine,
        in_specs=(
            P(DP, None),
            P(),
            P(),
            P(EX, None, DP),
            P(EX, None, DP),
            P(EX, DP, None),
            P(DP, None),
            P(DP, EX),
            P(EX, DP),
            P(EX, DP),
            P(DP, EX),
        ),
        out_specs=(P(EX, DP), P(EX, DP), P(DP, EX), P(DP, EX)),
        check_vma=False,
    )
```

```python
import math

import jax
import jax.numpy as jnp
from jax import lax
from jax.experimental import pallas as pl
from jax.experimental.pallas import tpu as pltpu
from jax.sharding import Mesh
from jax.sharding import PartitionSpec as P

NX, NZ, NY, NC = 4, 8, 4, 2
ND = NX * NZ
NE = NY * NC
DP = ("x", "z")
EX = ("y", "c")
BF = jnp.bfloat16
F32 = jnp.float32
VMEM_BYTES = 60 * 1024 * 1024
STEPS = 4


def exchange(values, axes):
    return lax.all_to_all(values, axes, 0, 0, tiled=False)


def spread(values, axes, count):
    return exchange(jnp.broadcast_to(values[None], (count,) + values.shape), axes)


def swap_cores(values):
    return lax.ppermute(values, "c", [(0, 1), (1, 0)])


def along_y(values, shift):
    return lax.ppermute(values, "y", [(i, (i + shift) % NY) for i in range(NY)])


def core_sum(values, core):
    half = values.shape[0] // 2
    low, high = values[:half], values[half:]
    give = jnp.where(core == 0, high, low).astype(BF)
    keep = jnp.where(core == 0, low, high)
    return (keep + swap_cores(give).astype(F32)).astype(BF)


def row_sum(mine, beside):
    others = [along_y(mine, s) for s in range(1, NY)]
    others, beside = lax.optimization_barrier((others, beside))
    total = mine.astype(F32)
    for term in others:
        total = total + term.astype(F32)
    total = total.astype(BF)
    return total, swap_cores(total), beside


def in_order(mine, other, core):
    first = jnp.where(core == 0, mine, other)
    second = jnp.where(core == 0, other, mine)
    return jnp.concatenate([first, second], axis=0)


def dot(a, b):
    return jnp.dot(a, b, preferred_element_type=F32)


def dot_tn(a, b):
    return lax.dot_general(a, b, (((0,), (0,)), ((), ())), preferred_element_type=F32)


def dot_nt(a, b):
    return lax.dot_general(a, b, (((1,), (1,)), ((), ())), preferred_element_type=F32)


def two_parts(core, chunk):
    mine = pl.multiple_of(core * chunk, 256)
    rest = pl.multiple_of((1 - core) * chunk, 256)
    return pl.ds(mine, chunk), pl.ds(rest, chunk)


def weight_copies(where_ref, j, hbm_refs, buffers, sems):
    depth = buffers[0].shape[1]
    start = pl.multiple_of(where_ref[j] * depth, 512)
    return [
        pltpu.make_async_copy(src.at[0, pl.ds(start, depth), :], buf.at[j], sems.at[i, j])
        for i, (src, buf) in enumerate(zip(hbm_refs, buffers))
    ]


def products(a, b, spot, wg, wu, rt, core):
    chunk = a.shape[1]
    mine, rest = two_parts(core, chunk)
    base = spot * (2 * chunk)
    r0 = rt[:, pl.ds(pl.multiple_of(base + core * chunk, 256), chunk)]
    r1 = rt[:, pl.ds(pl.multiple_of(base + (1 - core) * chunk, 256), chunk)]
    return (
        dot(a, wg[mine, :]) + dot(b, wg[rest, :]),
        dot(a, wu[mine, :]) + dot(b, wu[rest, :]),
        dot_nt(a, r0) + dot_nt(b, r1),
    )


def expert_kernel(*refs):
    xs = refs[:8]
    wg, wu, rt, ids, wd = refs[8:13]
    keeps = refs[13:17]
    gives = refs[17:21]
    xbuf, gbuf, ubuf, dbuf, hidden, block, obuf, xsems, sems, dsems, osems = refs[21:]
    outs = tuple(keeps) + tuple(gives)
    row = lax.axis_index("y")
    core = lax.axis_index("c")
    where = [row] + [lax.rem(row - s + NY, NY) for s in (1, 3, 2)]
    copies = [weight_copies(where, j, (wg, wu), (gbuf, ubuf), sems) for j in range(NY)]
    rows = dbuf.shape[1]
    downs = [
        pltpu.make_async_copy(wd.at[pl.ds(j * rows, rows), :], dbuf.at[j], dsems.at[j])
        for j in range(STEPS)
    ]
    arrivals = [
        pltpu.make_async_copy(xs[i], xbuf.at[i], xsems.at[i]) for i in range(len(xs))
    ]
    for j in range(NY):
        for copy in copies[j] + arrivals[2 * j : 2 * j + 2]:
            copy.start()
    for copy in downs:
        copy.start()
    g = u = logits = None
    for j in range(NY):
        for copy in copies[j] + arrivals[2 * j : 2 * j + 2]:
            copy.wait()
        gate, up, logit = products(
            xbuf[2 * j], xbuf[2 * j + 1], where[j], gbuf.at[j], ubuf.at[j], rt, core
        )
        if j == 0:
            g, u, logits = gate, up, logit
        else:
            g, u, logits = g + gate, u + up, logits + logit

    expert = row * NC + core
    lane = lax.broadcasted_iota(jnp.int32, logits.shape, 1)
    first = ids[:, 0:1]
    second = ids[:, 1:2]
    l0 = jnp.sum(jnp.where(lane == first, logits, 0.0), axis=1, keepdims=True)
    l1 = jnp.sum(jnp.where(lane == second, logits, 0.0), axis=1, keepdims=True)
    gate = jnp.where(first == expert, jax.nn.sigmoid(l0 - l1), 0.0) + jnp.where(
        second == expert, jax.nn.sigmoid(l1 - l0), 0.0
    )
    named = (first == expert) | (second == expert)
    active = jnp.where(named, g * jax.nn.sigmoid(g) * u * gate, 0.0)
    half = active.shape[0] // 2
    low = active[:half]
    high = active[half:]
    hidden[:half] = jnp.where(core == 0, low, high).astype(BF)
    hidden[half:] = jnp.where(core == 0, high, low).astype(BF)

    count = block.shape[0]
    leaving = []
    for j in range(STEPS):
        downs[j].wait()
        res = dot_nt(dbuf[j], hidden[...])
        block[...] = res.astype(BF).reshape(block.shape)
        span = pl.ds(j * count, count)
        for s in range(NY):
            at = lax.rem(row + s, NY)
            obuf[s, span] = block[:, at, :, :half]
            obuf[NY + s, span] = block[:, at, :, half:]
        for i in range(2 * NY):
            leave = pltpu.make_async_copy(
                obuf.at[i, span], outs[i].at[span], osems.at[i, j]
            )
            leave.start()
            leaving.append(leave)
    for leave in leaving:
        leave.wait()


IN_VMEM = pl.BlockSpec(memory_space=pltpu.VMEM)
IN_HBM = pl.BlockSpec(memory_space=pltpu.HBM)
IN_ANY = pl.BlockSpec(memory_space=pl.ANY)


def first_kernel(teacher, student, out, part, own, sems):
    chunk = part.shape[1]
    place = lax.axis_index("y") * NC + lax.axis_index("c")
    start = pl.multiple_of(place * chunk, 256)
    copies = [
        pltpu.make_async_copy(teacher.at[:, pl.ds(start, chunk)], part, sems.at[0]),
        pltpu.make_async_copy(student, own, sems.at[1]),
    ]
    for copy in copies:
        copy.start()
    for copy in copies:
        copy.wait()
    for d in range(ND):
        out[d, :, :chunk] = part[...]
        out[d, :, chunk:] = own[...]


def first_payload(teacher_in, student_in, chunk):
    rows, cols = student_in.shape
    return pl.pallas_call(
        first_kernel,
        out_shape=jax.ShapeDtypeStruct((ND, rows, chunk + cols), BF),
        in_specs=[IN_ANY, IN_ANY],
        out_specs=IN_VMEM,
        scratch_shapes=[
            pltpu.VMEM((rows, chunk), BF),
            pltpu.VMEM((rows, cols), BF),
            pltpu.SemaphoreType.DMA((2,)),
        ],
        compiler_params=pltpu.CompilerParams(vmem_limit_bytes=VMEM_BYTES),
    )(teacher_in, student_in)


def expert_products(xs, w_gate, w_up, router_t, ids, down_t, tokens, chunk):
    hid = w_gate.shape[2]
    width = down_t.shape[0]
    group = width // (ND * NY)
    out = jax.ShapeDtypeStruct((ND, group, tokens // 2), BF)
    return pl.pallas_call(
        expert_kernel,
        out_shape=(out,) * 8,
        in_specs=[IN_ANY] * 8
        + [IN_HBM, IN_HBM, IN_VMEM, IN_VMEM, IN_HBM],
        out_specs=[IN_ANY] * 8,
        scratch_shapes=[
            pltpu.VMEM((NE, tokens, chunk), BF),
            pltpu.VMEM((NY, 2 * chunk, hid), BF),
            pltpu.VMEM((NY, 2 * chunk, hid), BF),
            pltpu.VMEM((STEPS, width // STEPS, hid), BF),
            pltpu.VMEM((tokens, hid), BF),
            pltpu.VMEM((ND // STEPS, NY, group, tokens), BF),
            pltpu.VMEM((2 * NY, ND, group, tokens // 2), BF),
            pltpu.SemaphoreType.DMA((NE,)),
            pltpu.SemaphoreType.DMA((2, NY)),
            pltpu.SemaphoreType.DMA((STEPS,)),
            pltpu.SemaphoreType.DMA((2 * NY, STEPS)),
        ],
        compiler_params=pltpu.CompilerParams(vmem_limit_bytes=VMEM_BYTES),
        cost_estimate=pl.CostEstimate(
            flops=4 * tokens * NE * chunk * hid + 2 * tokens * hid * width,
            bytes_accessed=2 * NE * chunk * (2 * hid + tokens) + 2 * width * (hid + tokens),
            transcendentals=tokens * hid,
        ),
    )(*xs, w_gate, w_up, router_t, ids, down_t)


def grad_kernel(own, other, gate, up, student, gate_grad, up_grad):
    half = own.shape[0]
    core = lax.axis_index("c")
    total_gate = None
    for side, d_ref in enumerate((own, other)):
        at = core if side == 0 else 1 - core
        rows = pl.ds(pl.multiple_of(at * half, 128), half)
        d_hidden = d_ref[...].astype(F32)
        g = gate[rows, :]
        sigma = jax.nn.sigmoid(g)
        d_gate = (d_hidden * up[rows, :] * sigma * (1.0 + g * (1.0 - sigma))).astype(BF)
        d_up = (d_hidden * (g * sigma)).astype(BF)
        tokens = student[rows, :]
        if side == 0:
            total_gate = dot_tn(d_gate, tokens)
            total_up = dot_tn(d_up, tokens)
        else:
            gate_grad[...] = (total_gate + dot_tn(d_gate, tokens)).astype(BF)
            up_grad[...] = (total_up + dot_tn(d_up, tokens)).astype(BF)


def weight_grads(own, other, gate_s, up_s, student_all):
    out = jax.ShapeDtypeStruct((gate_s.shape[1], student_all.shape[1]), BF)
    return pl.pallas_call(
        grad_kernel,
        out_shape=(out, out),
        in_specs=[pl.BlockSpec(memory_space=pltpu.VMEM)] * 5,
        out_specs=[pl.BlockSpec(memory_space=pltpu.VMEM)] * 2,
        compiler_params=pltpu.CompilerParams(vmem_limit_bytes=16 * 1024 * 1024),
    )(own, other, gate_s, up_s, student_all)


def body(
    teacher_in,
    route_ids,
    router,
    w_gate,
    w_up,
    w_down,
    projection,
    student_in,
    s_gate,
    s_up,
    s_down,
):
    core = lax.axis_index("c")
    row = lax.axis_index("y")
    expert = row * NC + core
    tok_dp, width = teacher_in.shape
    tokens = route_ids.shape[0]
    sff_dev = s_gate.shape[1]
    sd_dev = student_in.shape[1]
    chunk = width // NE
    half = tokens // 2
    group = width // (ND * NY)

    sent = first_payload(teacher_in, student_in, chunk)
    arrived = exchange(sent, DP).reshape(tokens, chunk + sd_dev)
    arrived, down_t = lax.optimization_barrier((arrived, w_down[0].T))
    own = arrived[:, :chunk]
    student_all = arrived[:, chunk:]
    router_t = router.T

    far = [along_y(own, s) for s in range(1, NY)]
    own_other = swap_cores(own)
    far_other = [swap_cores(v) for v in far]
    xs = [own, own_other]
    for s in (1, 3, 2):
        xs += [far[s - 1], far_other[s - 1]]
    parts = expert_products(
        xs, w_gate, w_up, router_t, route_ids, down_t, tokens, chunk
    )
    pair_mine = core_sum(
        jnp.concatenate([dot(student_all, s_gate), dot(student_all, s_up)], axis=1), core
    )
    keeps, gives = parts[:4], parts[4:]

    arriving = []
    mine = None
    for s in (2, 1, 3, 0):
        both = (keeps[s].astype(F32) + swap_cores(gives[s]).astype(F32)).astype(BF)
        if s:
            arriving.append(along_y(both, s))
        else:
            mine = both
    total = mine.astype(F32)
    for term in arriving:
        total = total + term.astype(F32)
    terms = exchange(total.astype(BF), DP)
    pair_mine, pair_other, _ = row_sum(pair_mine, row)
    pair_sums = in_order(pair_mine, pair_other, core).astype(F32)
    gate_s = pair_sums[:, :sff_dev]
    up_s = pair_sums[:, sff_dev:]
    hidden_s = (gate_s * jax.nn.sigmoid(gate_s) * up_s).astype(BF)
    student_part = dot(hidden_s, s_down)
    summed = jnp.sum(terms.astype(F32), axis=0).astype(BF)
    pieces = [summed] + [along_y(summed, s) for s in range(1, NY)]
    mine = jnp.concatenate(pieces, axis=0)
    other = swap_cores(mine)
    cols = lax.dynamic_slice_in_dim(projection, expert * sd_dev, sd_dev, 1)
    cols = jnp.concatenate(
        [
            lax.dynamic_slice_in_dim(cols, lax.rem(row - s + NY, NY) * group, group, 0)
            for s in range(NY)
        ],
        axis=0,
    )
    first = jnp.where(core == 0, mine, other)
    second = jnp.where(core == 0, other, mine)
    target = dot_tn(jnp.concatenate([first, second], axis=1), cols)

    out_part = (student_part - target).astype(BF)
    terms = exchange(out_part.reshape(ND, tok_dp, sd_dev), DP)
    mismatch = student_in.astype(F32) + jnp.sum(terms.astype(F32), axis=0)
    cotangent = (mismatch * (1.0 / math.sqrt(tokens))).astype(BF)
    cotangent_all = spread(cotangent, DP, ND).reshape(tokens, sd_dev)
    grad_down = dot_tn(hidden_s, cotangent_all).astype(BF)
    d_mine, d_other, grad_down = row_sum(
        core_sum(dot_nt(cotangent_all, s_down), core), grad_down
    )
    grad_gate, grad_up = weight_grads(d_mine, d_other, gate_s, up_s, student_all)
    grad_gate = grad_gate.T
    grad_up = grad_up.T
    return (grad_gate, grad_up, grad_down, mismatch)


def solution(mesh):
    fine = Mesh(mesh.devices.reshape(NX, NZ, NY, NC), ("x", "z", "y", "c"))
    return jax.shard_map(
        body,
        mesh=fine,
        in_specs=(
            P(DP, None),
            P(),
            P(),
            P(EX, None, DP),
            P(EX, None, DP),
            P(EX, DP, None),
            P(DP, None),
            P(DP, EX),
            P(EX, DP),
            P(EX, DP),
            P(DP, EX),
        ),
        out_specs=(P(EX, DP), P(EX, DP), P(DP, EX), P(DP, EX)),
        check_vma=False,
    )
```

```python
import math

import jax
import jax.numpy as jnp
from jax import lax
from jax.experimental import pallas as pl
from jax.experimental.pallas import tpu as pltpu
from jax.sharding import Mesh
from jax.sharding import PartitionSpec as P

NX, NZ, NY, NC = 4, 8, 4, 2
ND = NX * NZ
NE = NY * NC
DP = ("x", "z")
EX = ("y", "c")
BF = jnp.bfloat16
F32 = jnp.float32
VMEM_BYTES = 60 * 1024 * 1024
STEPS = 8


def exchange(values, axes):
    return lax.all_to_all(values, axes, 0, 0, tiled=False)


def spread(values, axes, count):
    return exchange(jnp.broadcast_to(values[None], (count,) + values.shape), axes)


def swap_cores(values):
    return lax.ppermute(values, "c", [(0, 1), (1, 0)])


def along_y(values, shift):
    return lax.ppermute(values, "y", [(i, (i + shift) % NY) for i in range(NY)])


def core_sum(values, core):
    half = values.shape[0] // 2
    low, high = values[:half], values[half:]
    give = jnp.where(core == 0, high, low).astype(BF)
    keep = jnp.where(core == 0, low, high)
    return (keep + swap_cores(give).astype(F32)).astype(BF)


def row_sum(mine, beside):
    others = [along_y(mine, s) for s in range(1, NY)]
    others, beside = lax.optimization_barrier((others, beside))
    total = mine.astype(F32)
    for term in others:
        total = total + term.astype(F32)
    total = total.astype(BF)
    return total, swap_cores(total), beside


def in_order(mine, other, core):
    first = jnp.where(core == 0, mine, other)
    second = jnp.where(core == 0, other, mine)
    return jnp.concatenate([first, second], axis=0)


def dot(a, b):
    return jnp.dot(a, b, preferred_element_type=F32)


def dot_tn(a, b):
    return lax.dot_general(a, b, (((0,), (0,)), ((), ())), preferred_element_type=F32)


def dot_nt(a, b):
    return lax.dot_general(a, b, (((1,), (1,)), ((), ())), preferred_element_type=F32)


def two_parts(core, chunk):
    mine = pl.multiple_of(core * chunk, 256)
    rest = pl.multiple_of((1 - core) * chunk, 256)
    return pl.ds(mine, chunk), pl.ds(rest, chunk)


def weight_copies(where_ref, j, hbm_refs, buffers, sems):
    depth = buffers[0].shape[1]
    start = pl.multiple_of(where_ref[j] * depth, 512)
    return [
        pltpu.make_async_copy(src.at[0, pl.ds(start, depth), :], buf.at[j], sems.at[i, j])
        for i, (src, buf) in enumerate(zip(hbm_refs, buffers))
    ]


def products(a, b, spot, wg, wu, rt, core):
    chunk = a.shape[1]
    mine, rest = two_parts(core, chunk)
    base = spot * (2 * chunk)
    r0 = rt[:, pl.ds(pl.multiple_of(base + core * chunk, 256), chunk)]
    r1 = rt[:, pl.ds(pl.multiple_of(base + (1 - core) * chunk, 256), chunk)]
    return (
        dot(a, wg[mine, :]) + dot(b, wg[rest, :]),
        dot(a, wu[mine, :]) + dot(b, wu[rest, :]),
        dot_nt(a, r0) + dot_nt(b, r1),
    )


def expert_kernel(*refs):
    xs = refs[:8]
    wg, wu, rt, ids, wd = refs[8:13]
    keeps = refs[13:17]
    gives = refs[17:21]
    xbuf, gbuf, ubuf, dbuf, hidden, block, obuf, xsems, sems, dsems, osems = refs[21:]
    outs = tuple(keeps) + tuple(gives)
    row = lax.axis_index("y")
    core = lax.axis_index("c")
    where = [row] + [lax.rem(row - s + NY, NY) for s in (1, 3, 2)]
    copies = [weight_copies(where, j, (wg, wu), (gbuf, ubuf), sems) for j in range(NY)]
    rows = dbuf.shape[1]
    downs = [
        pltpu.make_async_copy(wd.at[pl.ds(j * rows, rows), :], dbuf.at[j], dsems.at[j])
        for j in range(STEPS)
    ]
    arrivals = [
        pltpu.make_async_copy(xs[i], xbuf.at[i], xsems.at[i]) for i in range(len(xs))
    ]
    for j in range(NY):
        for copy in copies[j] + arrivals[2 * j : 2 * j + 2]:
            copy.start()
    for copy in downs:
        copy.start()
    g = u = logits = None
    for j in range(NY):
        for copy in copies[j] + arrivals[2 * j : 2 * j + 2]:
            copy.wait()
        gate, up, logit = products(
            xbuf[2 * j], xbuf[2 * j + 1], where[j], gbuf.at[j], ubuf.at[j], rt, core
        )
        if j == 0:
            g, u, logits = gate, up, logit
        else:
            g, u, logits = g + gate, u + up, logits + logit

    expert = row * NC + core
    lane = lax.broadcasted_iota(jnp.int32, logits.shape, 1)
    first = ids[:, 0:1]
    second = ids[:, 1:2]
    l0 = jnp.sum(jnp.where(lane == first, logits, 0.0), axis=1, keepdims=True)
    l1 = jnp.sum(jnp.where(lane == second, logits, 0.0), axis=1, keepdims=True)
    gate = jnp.where(first == expert, jax.nn.sigmoid(l0 - l1), 0.0) + jnp.where(
        second == expert, jax.nn.sigmoid(l1 - l0), 0.0
    )
    named = (first == expert) | (second == expert)
    active = jnp.where(named, g * jax.nn.sigmoid(g) * u * gate, 0.0)
    half = active.shape[0] // 2
    low = active[:half]
    high = active[half:]
    hidden[:half] = jnp.where(core == 0, low, high).astype(BF)
    hidden[half:] = jnp.where(core == 0, high, low).astype(BF)

    count = block.shape[0]
    leaving = []
    for j in range(STEPS):
        downs[j].wait()
        res = dot_nt(dbuf[j], hidden[...])
        block[...] = res.astype(BF).reshape(block.shape)
        span = pl.ds(j * count, count)
        for s in range(NY):
            at = lax.rem(row + s, NY)
            obuf[s, span] = block[:, at, :, :half]
            obuf[NY + s, span] = block[:, at, :, half:]
        for i in range(2 * NY):
            leave = pltpu.make_async_copy(
                obuf.at[i, span], outs[i].at[span], osems.at[i, j]
            )
            leave.start()
            leaving.append(leave)
    for leave in leaving:
        leave.wait()


IN_VMEM = pl.BlockSpec(memory_space=pltpu.VMEM)
IN_HBM = pl.BlockSpec(memory_space=pltpu.HBM)
IN_ANY = pl.BlockSpec(memory_space=pl.ANY)


def first_kernel(teacher, student, out, part, own, sems):
    chunk = part.shape[1]
    place = lax.axis_index("y") * NC + lax.axis_index("c")
    start = pl.multiple_of(place * chunk, 256)
    copies = [
        pltpu.make_async_copy(teacher.at[:, pl.ds(start, chunk)], part, sems.at[0]),
        pltpu.make_async_copy(student, own, sems.at[1]),
    ]
    for copy in copies:
        copy.start()
    for copy in copies:
        copy.wait()
    for d in range(ND):
        out[d, :, :chunk] = part[...]
        out[d, :, chunk:] = own[...]


def first_payload(teacher_in, student_in, chunk):
    rows, cols = student_in.shape
    return pl.pallas_call(
        first_kernel,
        out_shape=jax.ShapeDtypeStruct((ND, rows, chunk + cols), BF),
        in_specs=[IN_ANY, IN_ANY],
        out_specs=IN_VMEM,
        scratch_shapes=[
            pltpu.VMEM((rows, chunk), BF),
            pltpu.VMEM((rows, cols), BF),
            pltpu.SemaphoreType.DMA((2,)),
        ],
        compiler_params=pltpu.CompilerParams(vmem_limit_bytes=VMEM_BYTES),
    )(teacher_in, student_in)


def expert_products(xs, w_gate, w_up, router_t, ids, down_t, tokens, chunk):
    hid = w_gate.shape[2]
    width = down_t.shape[0]
    group = width // (ND * NY)
    out = jax.ShapeDtypeStruct((ND, group, tokens // 2), BF)
    return pl.pallas_call(
        expert_kernel,
        out_shape=(out,) * 8,
        in_specs=[IN_ANY] * 8
        + [IN_HBM, IN_HBM, IN_VMEM, IN_VMEM, IN_HBM],
        out_specs=[IN_ANY] * 8,
        scratch_shapes=[
            pltpu.VMEM((NE, tokens, chunk), BF),
            pltpu.VMEM((NY, 2 * chunk, hid), BF),
            pltpu.VMEM((NY, 2 * chunk, hid), BF),
            pltpu.VMEM((STEPS, width // STEPS, hid), BF),
            pltpu.VMEM((tokens, hid), BF),
            pltpu.VMEM((ND // STEPS, NY, group, tokens), BF),
            pltpu.VMEM((2 * NY, ND, group, tokens // 2), BF),
            pltpu.SemaphoreType.DMA((NE,)),
            pltpu.SemaphoreType.DMA((2, NY)),
            pltpu.SemaphoreType.DMA((STEPS,)),
            pltpu.SemaphoreType.DMA((2 * NY, STEPS)),
        ],
        compiler_params=pltpu.CompilerParams(vmem_limit_bytes=VMEM_BYTES),
        cost_estimate=pl.CostEstimate(
            flops=4 * tokens * NE * chunk * hid + 2 * tokens * hid * width,
            bytes_accessed=2 * NE * chunk * (2 * hid + tokens) + 2 * width * (hid + tokens),
            transcendentals=tokens * hid,
        ),
    )(*xs, w_gate, w_up, router_t, ids, down_t)


def grad_kernel(own, other, gate, up, student, gate_grad, up_grad):
    half = own.shape[0]
    core = lax.axis_index("c")
    total_gate = None
    for side, d_ref in enumerate((own, other)):
        at = core if side == 0 else 1 - core
        rows = pl.ds(pl.multiple_of(at * half, 128), half)
        d_hidden = d_ref[...].astype(F32)
        g = gate[rows, :]
        sigma = jax.nn.sigmoid(g)
        d_gate = (d_hidden * up[rows, :] * sigma * (1.0 + g * (1.0 - sigma))).astype(BF)
        d_up = (d_hidden * (g * sigma)).astype(BF)
        tokens = student[rows, :]
        if side == 0:
            total_gate = dot_tn(d_gate, tokens)
            total_up = dot_tn(d_up, tokens)
        else:
            gate_grad[...] = (total_gate + dot_tn(d_gate, tokens)).astype(BF)
            up_grad[...] = (total_up + dot_tn(d_up, tokens)).astype(BF)


def weight_grads(own, other, gate_s, up_s, student_all):
    out = jax.ShapeDtypeStruct((gate_s.shape[1], student_all.shape[1]), BF)
    return pl.pallas_call(
        grad_kernel,
        out_shape=(out, out),
        in_specs=[pl.BlockSpec(memory_space=pltpu.VMEM)] * 5,
        out_specs=[pl.BlockSpec(memory_space=pltpu.VMEM)] * 2,
        compiler_params=pltpu.CompilerParams(vmem_limit_bytes=16 * 1024 * 1024),
    )(own, other, gate_s, up_s, student_all)


def body(
    teacher_in,
    route_ids,
    router,
    w_gate,
    w_up,
    w_down,
    projection,
    student_in,
    s_gate,
    s_up,
    s_down,
):
    core = lax.axis_index("c")
    row = lax.axis_index("y")
    expert = row * NC + core
    tok_dp, width = teacher_in.shape
    tokens = route_ids.shape[0]
    sff_dev = s_gate.shape[1]
    sd_dev = student_in.shape[1]
    chunk = width // NE
    half = tokens // 2
    group = width // (ND * NY)

    sent = first_payload(teacher_in, student_in, chunk)
    arrived = exchange(sent, DP).reshape(tokens, chunk + sd_dev)
    arrived, down_t = lax.optimization_barrier((arrived, w_down[0].T))
    own = arrived[:, :chunk]
    student_all = arrived[:, chunk:]
    router_t = router.T

    far = [along_y(own, s) for s in range(1, NY)]
    own_other = swap_cores(own)
    far_other = [swap_cores(v) for v in far]
    xs = [own, own_other]
    for s in (1, 3, 2):
        xs += [far[s - 1], far_other[s - 1]]
    parts = expert_products(
        xs, w_gate, w_up, router_t, route_ids, down_t, tokens, chunk
    )
    pair_mine = core_sum(
        jnp.concatenate([dot(student_all, s_gate), dot(student_all, s_up)], axis=1), core
    )
    keeps, gives = parts[:4], parts[4:]

    arriving = []
    mine = None
    for s in (2, 1, 3, 0):
        both = (keeps[s].astype(F32) + swap_cores(gives[s]).astype(F32)).astype(BF)
        if s:
            arriving.append(along_y(both, s))
        else:
            mine = both
    total = mine.astype(F32)
    for term in arriving:
        total = total + term.astype(F32)
    terms = exchange(total.astype(BF), DP)
    pair_mine, pair_other, _ = row_sum(pair_mine, row)
    pair_sums = in_order(pair_mine, pair_other, core).astype(F32)
    gate_s = pair_sums[:, :sff_dev]
    up_s = pair_sums[:, sff_dev:]
    hidden_s = (gate_s * jax.nn.sigmoid(gate_s) * up_s).astype(BF)
    student_part = dot(hidden_s, s_down)
    summed = jnp.sum(terms.astype(F32), axis=0).astype(BF)
    pieces = [summed] + [along_y(summed, s) for s in range(1, NY)]
    mine = jnp.concatenate(pieces, axis=0)
    other = swap_cores(mine)
    cols = lax.dynamic_slice_in_dim(projection, expert * sd_dev, sd_dev, 1)
    cols = jnp.concatenate(
        [
            lax.dynamic_slice_in_dim(cols, lax.rem(row - s + NY, NY) * group, group, 0)
            for s in range(NY)
        ],
        axis=0,
    )
    first = jnp.where(core == 0, mine, other)
    second = jnp.where(core == 0, other, mine)
    target = dot_tn(jnp.concatenate([first, second], axis=1), cols)

    out_part = (student_part - target).astype(BF)
    terms = exchange(out_part.reshape(ND, tok_dp, sd_dev), DP)
    mismatch = student_in.astype(F32) + jnp.sum(terms.astype(F32), axis=0)
    cotangent = (mismatch * (1.0 / math.sqrt(tokens))).astype(BF)
    cotangent_all = spread(cotangent, DP, ND).reshape(tokens, sd_dev)
    grad_down = dot_tn(hidden_s, cotangent_all).astype(BF)
    d_mine, d_other, grad_down = row_sum(
        core_sum(dot_nt(cotangent_all, s_down), core), grad_down
    )
    grad_gate, grad_up = weight_grads(d_mine, d_other, gate_s, up_s, student_all)
    grad_gate = grad_gate.T
    grad_up = grad_up.T
    return (grad_gate, grad_up, grad_down, mismatch)


def solution(mesh):
    fine = Mesh(mesh.devices.reshape(NX, NZ, NY, NC), ("x", "z", "y", "c"))
    return jax.shard_map(
        body,
        mesh=fine,
        in_specs=(
            P(DP, None),
            P(),
            P(),
            P(EX, None, DP),
            P(EX, None, DP),
            P(EX, DP, None),
            P(DP, None),
            P(DP, EX),
            P(EX, DP),
            P(EX, DP),
            P(DP, EX),
        ),
        out_specs=(P(EX, DP), P(EX, DP), P(DP, EX), P(DP, EX)),
        check_vma=False,
    )
```
